32 devices in a mesh: blocks: 2 (over x), pencil: 4 (over y, core), tile: 4 (over z).
Axes of the slice: x: 2, y: 2, z: 4, core: 2. Of those that a mesh axis runs over, the one named last changes fastest.
Arguments:
- right_face: bfloat16 [8, 2, 2048, 2048], P(('blocks', 'tile'), None, 'pencil'), parts along dimension 0, may hold values from -6 to 6
- left_face: bfloat16 [8, 2, 2048, 2048], P(('blocks', 'tile'), None, 'pencil'), parts along dimension 0, may hold values from -6 to 6
- intersection_list: int32 [8, 3], P(('blocks', 'tile')), parts along dimension 0, may hold values from -64 to 64, as said below
- slice_ranges: int32 [8, 2], P(('blocks', 'tile')), parts along dimension 0, may hold values from 0 to 1, as said below
Outputs:
- maps: float32 [8, 2, 2048, 2048], P(('blocks', 'tile'), None, 'pencil'), parts along dimension 0
The draws below stay inside these ranges and needn't reach their ends.
There are 2 independent parts, one for each index of `blocks`. The reference program is written for one: setup_inputs(seed, part) draws one part's arguments, and reference() takes and returns one part's arrays. A program takes and returns all parts, laid end to end along the dimension named above; each array names one. Nothing has to cross between parts.
Inputs may be any that keep to these rules, and one draw needn't show every extreme that they name: `intersection_list`: column 0 is the intersection's width in slices, 1 to 2; it is 2 for some intersection and 1 for another. Columns 1 and 2 are coarse row and column offsets in pixels. `slice_ranges`: each first slice plus the intersection's width is at most 2.
All inputs are finite; a program needn't handle non-finite values.
Results may differ from the reference program's by a relative error of at most 0.0003.
Values may be sent and summed in bfloat16 or wider, within the bound.
A program may use at most 192 MiB of HBM per device.

```python
import math
import jax
import jax.numpy as jnp
from jax import lax

N1 = 2048
N2 = 2048
SL = 2
MAXOFF = 64
TILES = 4


def intersection_draw(key):
    keys = jax.random.split(key, 6)
    order = jnp.arange(TILES, dtype=jnp.int32)
    widths = jax.random.randint(keys[0], (TILES,), 1, SL + 1)
    full_tile = jax.random.randint(keys[1], (), 0, TILES)
    single_tile = (full_tile + 1 + jax.random.randint(keys[2], (), 0, TILES - 1)) % TILES
    widths = jnp.where(order == full_tile, SL, widths)
    widths = jnp.where(order == single_tile, 1, widths)
    spare_room = SL - widths
    start_near = jax.random.randint(keys[3], (TILES,), 0, spare_room + 1)
    start_near = jnp.where(order == single_tile, SL - 1, start_near)
    start_far = jax.random.randint(keys[4], (TILES,), 0, spare_room + 1)
    offsets = jax.random.randint(keys[5], (TILES, 2), 0 - MAXOFF, MAXOFF + 1)
    shift_rows = jnp.where(order == full_tile, MAXOFF, offsets[:, 0])
    shift_cols = jnp.where(order == single_tile, 0 - MAXOFF, offsets[:, 1])
    return (widths, shift_rows, shift_cols, start_near, start_far)


def draw_intersection_list(key, part):
    widths, shift_rows, shift_cols, start_near, start_far = intersection_draw(key)
    return jnp.stack([widths, shift_rows, shift_cols], axis=1).astype(jnp.int32)


def draw_slice_ranges(key, part):
    widths, shift_rows, shift_cols, start_near, start_far = intersection_draw(key)
    return jnp.stack([start_near, start_far], axis=1).astype(jnp.int32)


def level_of(key, extent, cuts, smallest, high):
    def one(dim, blocks):
        draws = jax.random.uniform(jax.random.fold_in(jax.random.fold_in(key, 6), dim), (blocks,), jnp.float32, smallest / len(cuts), high / len(cuts))
        return jnp.repeat(jnp.exp(draws), extent[dim] // blocks).reshape((-1,) + (1,) * (len(extent) - dim - 1))

    level = one(*cuts[0])
    for cut in cuts[1:]:
        level = level * one(*cut)
    return level


def gaussian(rng, extent, spread, most, cuts=(), held_as=jnp.bfloat16):
    array = jax.random.normal(rng, extent, jnp.float32) * spread
    if len(cuts) > 0:
        array = level_of(rng, extent, cuts, -0.22, 0.18) * array
    return jnp.clip(array, min=-most, max=most).astype(held_as)


def setup_inputs(seed: int = 0, part: int = 0) -> dict:
    splits = jax.random.split(jax.random.key(seed), 5)
    part_keys = jax.random.split(jax.random.fold_in(splits[4], part), 5)
    return {
        "right_face": gaussian(part_keys[0], (TILES, SL, N1, N2), 1.0, 6.0, ((0, 4), (2, 4))),
        "left_face": gaussian(part_keys[1], (TILES, SL, N1, N2), 1.0, 6.0, ((0, 4), (2, 4))),
        "intersection_list": draw_intersection_list(jax.random.fold_in(jax.random.fold_in(splits[4], part), 71), part),
        "slice_ranges": draw_slice_ranges(jax.random.fold_in(jax.random.fold_in(splits[4], part), 71), part),
    }


REG = 0.25

def reference(right_face, left_face, intersection_list, slice_ranges):
    neighbour = jnp.roll(left_face, -1, axis=0)
    height = right_face.shape[2]
    width = right_face.shape[3]
    scale = REG * height * width
    row_freq = jnp.arange(height, dtype=jnp.int32)[:, None]
    col_freq = jnp.arange(width, dtype=jnp.int32)[None, :]

    def one_intersection(inputs):
        right_slices, far_slices, info, ranges = inputs

        def accumulate(totals, step):
            near_image = lax.dynamic_index_in_dim(right_slices, jnp.minimum(ranges[0] + step, SL - 1), 0, keepdims=False)
            far_image = lax.dynamic_index_in_dim(far_slices, jnp.minimum(ranges[1] + step, SL - 1), 0, keepdims=False)
            near_spec = jnp.fft.fft2(near_image.astype(jnp.float32))
            far_spec = jnp.fft.fft2(far_image.astype(jnp.float32))
            product = near_spec * jnp.conj(far_spec)
            weight = 1.0 / (jnp.abs(product) + scale)
            live = step < info[0]
            new_real = totals[0] + jnp.where(live, jnp.real(product) * weight, 0.0)
            new_imag = totals[1] + jnp.where(live, jnp.imag(product) * weight, 0.0)
            return ((new_real, new_imag), None)
        zeros = jnp.zeros((height, width), jnp.float32)
        totals, unused = lax.scan(accumulate, (zeros, zeros), jnp.arange(SL, dtype=jnp.int32))
        inverse_count = 1.0 / info[0].astype(jnp.float32)
        mean_real = totals[0] * inverse_count
        mean_imag = totals[1] * inverse_count
        angle = (row_freq * info[1] % height).astype(jnp.float32) * (2.0 * math.pi / height) + (col_freq * info[2] % width).astype(jnp.float32) * (2.0 * math.pi / width)
        rotated_real = mean_real * jnp.cos(angle) - mean_imag * jnp.sin(angle)
        rotated_imag = mean_real * jnp.sin(angle) + mean_imag * jnp.cos(angle)
        field = jnp.fft.ifft2(rotated_real + 1j * rotated_imag)
        return (jnp.real(field) * math.sqrt(height * width)).astype(jnp.float32)
    corr = lax.map(one_intersection, (right_face, neighbour, intersection_list, slice_ranges))
    return jnp.stack([corr, jnp.roll(corr, 1, axis=0)], axis=1)
```

```python
import math

import jax
import jax.numpy as jnp
import ml_dtypes
import numpy as np
from jax import lax
from jax.sharding import PartitionSpec as P

REG = 0.25
CHUNKS = 2
HIGH = lax.Precision.HIGH


def shift_tile(value, steps):
    count = lax.axis_size("tile")
    return lax.ppermute(value, "tile", [(s, (s + steps) % count) for s in range(count)])


def swap_groups(value, members):
    count = 2 * members
    return lax.ppermute(value, "pencil", [(s, (s + members) % count) for s in range(count)])


def shift_members(value, members, steps):
    pairs = [
        (g * members + s, g * members + (s + steps) % members)
        for g in range(2)
        for s in range(members)
    ]
    return lax.ppermute(value, "pencil", pairs)


def hi_lo(table):
    high = table.astype(ml_dtypes.bfloat16)
    low = (table - high.astype(np.float64)).astype(ml_dtypes.bfloat16)
    return jnp.asarray(high), jnp.asarray(low)


def row_tables(width, members):
    half = width // 2
    columns = half // members
    x = np.arange(width)[:, None]
    l = np.arange(half)[None, :]
    angle = (x * l % width) * (2.0 * math.pi / width)
    cos_part, sin_part = np.cos(angle), -np.sin(angle)
    sin_part[:, 0] = 1.0 - 2.0 * (np.arange(width) % 2)
    forward = np.stack([cos_part, sin_part], axis=1)
    forward = forward.reshape(width, 2, members, columns).transpose(2, 0, 1, 3)
    forward = forward.reshape(members, width, 2 * columns)
    weight = np.where(np.arange(half) == 0, 1.0, 2.0)
    inverse = np.stack([cos_part * weight, sin_part * weight], axis=1)
    inverse = inverse.reshape(width, 2, members, columns).transpose(2, 1, 3, 0)
    inverse = inverse.reshape(members, 2 * columns, width)
    return forward, inverse


def column_table(quarter, sign):
    n = np.arange(quarter)
    angle = (n[:, None] * n[None, :] % quarter) * (2.0 * math.pi / quarter)
    c, s = np.cos(angle), sign * np.sin(angle)
    return np.block([[c, -s], [s, c]]).astype(np.float32)


def twist_table(height):
    quarter = height // 4
    angle = np.arange(4)[:, None] * np.arange(quarter)[None, :] * (2.0 * math.pi / height)
    return (
        np.cos(angle).astype(np.float32)[:, :, None],
        np.sin(angle).astype(np.float32)[:, :, None],
    )


def split(a, b):
    return jnp.einsum("ab,rbc->rac", a, b, precision=HIGH)


def mirrored(vec):
    flipped = vec[:, ::-1]
    return jnp.stack([jnp.roll(flipped[0], 1), flipped[3], flipped[2], flipped[1]])


def cross(nr, ni, fr, fi, scale):
    pr = nr * fr + ni * fi
    pi = ni * fr - nr * fi
    weight = 1.0 / (jnp.sqrt(pr * pr + pi * pi) + scale)
    return pr * weight, pi * weight


def rotate(ar, ai, br, bi):
    return ar * br - ai * bi, ar * bi + ai * br


def shards(right_face, left_face, intersection_list, slice_ranges):
    right = right_face[0]
    left = left_face[0]
    depth, rows, width = right.shape
    count = lax.axis_size("pencil")
    members = count // 2
    height = rows * count
    quarter = height // 4
    columns = width // (2 * members)
    scale = REG * height * width
    place = lax.axis_index("pencil")
    group = place // members
    member = place % members
    sign = (1 - 2 * group).astype(jnp.float32)

    live_count = intersection_list[0, 0]
    far_start = shift_tile(slice_ranges[:, 1:2], 1)[0, 0]

    def pick(slices, start, step):
        return lax.dynamic_index_in_dim(
            slices, jnp.minimum(start + step, depth - 1), 0, keepdims=False
        )

    near_start = slice_ranges[0, 0]
    right_keep = pick(right, near_start, group)
    right_send = pick(right, near_start, 1 - group)
    left_keep = pick(left, far_start, group)
    left_send = pick(left, far_start, 1 - group)
    left_got = swap_groups(left_send, members)
    far_own = shift_tile(left_keep, -1)
    right_got = swap_groups(right_send, members)
    far_other = shift_tile(left_got, -1)

    forward_np, inverse_np = row_tables(width, members)
    forward_hi, forward_lo = hi_lo(forward_np)
    table_hi = lax.dynamic_index_in_dim(forward_hi, member, 0, keepdims=False)
    table_lo = lax.dynamic_index_in_dim(forward_lo, member, 0, keepdims=False)

    def gathered(block):
        parts = [block] + [shift_members(block, members, s) for s in range(1, members)]
        if members == 2:
            first = member == 0
            ordered = [jnp.where(first, parts[0], parts[1]), jnp.where(first, parts[1], parts[0])]
            return jnp.concatenate(ordered, axis=0)
        order = (member - jnp.arange(members)) % members
        return jnp.take(jnp.stack(parts), order, axis=0).reshape(members * rows, width)

    def row_pass(block):
        pixels = gathered(block)
        spec = jnp.dot(pixels, table_hi, preferred_element_type=jnp.float32) + jnp.dot(
            pixels, table_lo, preferred_element_type=jnp.float32
        )
        return spec.reshape(2, quarter, 2 * columns)

    twist_cos, twist_sin = twist_table(height)
    forward_table = column_table(quarter, -1.0)

    def column_pass(own, other):
        even = own + other
        odd = (own - other) * sign
        er, ei = even[..., :columns], even[..., columns:]
        dr, di = odd[..., :columns], odd[..., columns:]
        zr = jnp.stack([er[0] + er[1], dr[0] + di[1], er[0] - er[1], dr[0] - di[1]])
        zi = jnp.stack([ei[0] + ei[1], di[0] - dr[1], ei[0] - ei[1], di[0] + dr[1]])
        zr, zi = rotate(zr, zi, twist_cos, -twist_sin)
        return split(forward_table, jnp.concatenate([zr, zi], axis=1))

    near = column_pass(row_pass(right_keep), row_pass(right_got))
    far = column_pass(row_pass(far_own), row_pass(far_other))
    nr, ni = near[:, :quarter], near[:, quarter:]
    fr, fi = far[:, :quarter], far[:, quarter:]

    factor = jnp.where(group < live_count, 1.0 / live_count.astype(jnp.float32), 0.0) * (
        1.0 / math.sqrt(height * width)
    )
    k = 4 * jnp.arange(quarter, dtype=jnp.int32)[None, :] + jnp.arange(4, dtype=jnp.int32)[:, None]
    angle_k = (k * intersection_list[0, 1] % height).astype(jnp.float32) * (2.0 * math.pi / height)
    kr, ki = jnp.cos(angle_k) * factor, jnp.sin(angle_k) * factor
    l = member * columns + jnp.arange(columns, dtype=jnp.int32)
    angle_l = (l * intersection_list[0, 2] % width).astype(jnp.float32) * (2.0 * math.pi / width)
    lr, li = jnp.cos(angle_l), jnp.sin(angle_l)

    pr, pi = cross(nr, ni, fr, fi, scale)
    pr, pi = rotate(pr, pi, kr[:, :, None], ki[:, :, None])
    pr, pi = rotate(pr, pi, lr, li)

    def unpack(vr, vi):
        mr, mi = mirrored(vr), mirrored(vi)
        return (
            0.5 * (vr + mr),
            0.5 * (vi - mi),
            0.5 * (vi + mi),
            0.5 * (mr - vr),
        )

    n0r, n0i, n1r, n1i = unpack(nr[:, :, 0], ni[:, :, 0])
    f0r, f0i, f1r, f1i = unpack(fr[:, :, 0], fi[:, :, 0])
    p0r, p0i = rotate(*cross(n0r, n0i, f0r, f0i, scale), kr, ki)
    p1r, p1i = rotate(*cross(n1r, n1i, f1r, f1i, scale), kr, ki)
    nyquist = (1 - 2 * ((width // 2 * intersection_list[0, 2] % width) // (width // 2))).astype(
        jnp.float32
    )
    packed_r = p0r - p1i * nyquist
    packed_i = p0i + p1r * nyquist
    first_column = jnp.logical_and(jnp.arange(columns) == 0, member == 0)
    pr = jnp.where(first_column, packed_r[:, :, None], pr)
    pi = jnp.where(first_column, packed_i[:, :, None], pi)

    waves = split(column_table(quarter, 1.0), jnp.concatenate([pr, pi], axis=1))
    ur, ui = rotate(waves[:, :quarter], waves[:, quarter:], twist_cos, twist_sin)
    even = jnp.stack(
        [
            jnp.concatenate([ur[0] + ur[2], ui[0] + ui[2]], axis=-1),
            jnp.concatenate([ur[0] - ur[2], ui[0] - ui[2]], axis=-1),
        ]
    )
    odd = sign * jnp.stack(
        [
            jnp.concatenate([ur[1] + ur[3], ui[1] + ui[3]], axis=-1),
            jnp.concatenate([ui[3] - ui[1], ur[1] - ur[3]], axis=-1),
        ]
    )
    own = (even + odd).reshape(members, rows, 2 * columns)
    other = (even - odd).reshape(members, rows, 2 * columns)

    inverse_table = jnp.asarray(inverse_np.astype(np.float32))
    own_parts, other_parts = [], []
    step = rows // CHUNKS
    for c in range(CHUNKS):
        cut = slice(c * step, (c + 1) * step)
        total = own[:, cut] + swap_groups(other[:, cut], members)
        result = None
        for s in range(members):
            target = (member + s) % members
            block = lax.dynamic_index_in_dim(total, target, 0, keepdims=False)
            if s > 0:
                block = shift_members(block, members, s)
            table = lax.dynamic_index_in_dim(
                inverse_table, (member - s) % members, 0, keepdims=False
            )
            term = jnp.dot(block, table, precision=HIGH)
            result = term if result is None else result + term
        own_parts.append(result)
        other_parts.append(shift_tile(result, 1))
    return jnp.stack([jnp.concatenate(own_parts), jnp.concatenate(other_parts)])[None]


def solution(mesh):
    faces = P(("blocks", "tile"), None, "pencil", None)
    lists = P(("blocks", "tile"), None)
    return jax.shard_map(
        shards,
        mesh=mesh,
        in_specs=(faces, faces, lists, lists),
        out_specs=faces,
        check_vma=False,
    )
```

```python
import math

import jax
import jax.numpy as jnp
import ml_dtypes
import numpy as np
from jax import lax
from jax.sharding import PartitionSpec as P

REG = 0.25
CHUNKS = 2
HIGH = lax.Precision.HIGH


def shift_tile(value, steps):
    count = lax.axis_size("tile")
    return lax.ppermute(value, "tile", [(s, (s + steps) % count) for s in range(count)])


def swap_groups(value, members):
    count = 2 * members
    return lax.ppermute(value, "pencil", [(s, (s + members) % count) for s in range(count)])


def shift_members(value, members, steps):
    pairs = [
        (g * members + s, g * members + (s + steps) % members)
        for g in range(2)
        for s in range(members)
    ]
    return lax.ppermute(value, "pencil", pairs)


def hi_lo(table):
    high = table.astype(ml_dtypes.bfloat16)
    low = (table - high.astype(np.float64)).astype(ml_dtypes.bfloat16)
    return jnp.asarray(high), jnp.asarray(low)


def row_tables(width, members):
    half = width // 2
    columns = half // members
    x = np.arange(width)[:, None]
    l = np.arange(half)[None, :]
    angle = (x * l % width) * (2.0 * math.pi / width)
    cos_part, sin_part = np.cos(angle), -np.sin(angle)
    sin_part[:, 0] = 1.0 - 2.0 * (np.arange(width) % 2)
    forward = np.stack([cos_part, sin_part], axis=1)
    forward = forward.reshape(width, 2, members, columns).transpose(2, 0, 1, 3)
    forward = forward.reshape(members, width, 2 * columns)
    weight = np.where(np.arange(half) == 0, 1.0, 2.0)
    inverse = np.stack([cos_part * weight, sin_part * weight], axis=1)
    inverse = inverse.reshape(width, 2, members, columns).transpose(2, 1, 3, 0)
    inverse = inverse.reshape(members, 2 * columns, width)
    return forward, inverse


def column_table(quarter, sign):
    n = np.arange(quarter)
    angle = (n[:, None] * n[None, :] % quarter) * (2.0 * math.pi / quarter)
    c, s = np.cos(angle), sign * np.sin(angle)
    return np.block([[c, -s], [s, c]]).astype(np.float32)


def twist_table(height):
    quarter = height // 4
    angle = np.arange(4)[:, None] * np.arange(quarter)[None, :] * (2.0 * math.pi / height)
    return (
        np.cos(angle).astype(np.float32)[:, :, None],
        np.sin(angle).astype(np.float32)[:, :, None],
    )


def split(a, b):
    return jnp.dot(a, b, precision=HIGH)


def encode(value):
    tall = value.shape[-2]
    group = math.gcd(tall, 64)
    grouped = value.reshape(value.shape[:-2] + (tall // group, group, value.shape[-1]))
    peak = jnp.maximum(jnp.max(jnp.abs(grouped), axis=-2, keepdims=True), 1e-30)
    coded = jnp.round(grouped * (32767.0 / peak)).astype(jnp.int16)
    return coded.reshape(value.shape), jnp.squeeze(peak, axis=-2) * (1.0 / 32767.0)


def decode(coded, scale):
    tall = coded.shape[-2]
    count = scale.shape[-2]
    grouped = coded.reshape(coded.shape[:-2] + (count, tall // count, coded.shape[-1]))
    return (grouped.astype(jnp.float32) * scale[..., None, :]).reshape(coded.shape)


def mirrored(vec):
    flipped = vec[:, ::-1]
    return jnp.stack([jnp.roll(flipped[0], 1), flipped[3], flipped[2], flipped[1]])


def cross(nr, ni, fr, fi, scale):
    pr = nr * fr + ni * fi
    pi = ni * fr - nr * fi
    weight = 1.0 / (jnp.sqrt(pr * pr + pi * pi) + scale)
    return pr * weight, pi * weight


def rotate(ar, ai, br, bi):
    return ar * br - ai * bi, ar * bi + ai * br


def shards(right_face, left_face, intersection_list, slice_ranges):
    right = right_face[0]
    left = left_face[0]
    depth, rows, width = right.shape
    count = lax.axis_size("pencil")
    members = count // 2
    height = rows * count
    quarter = height // 4
    columns = width // (2 * members)
    scale = REG * height * width
    place = lax.axis_index("pencil")
    group = place // members
    member = place % members
    sign = (1 - 2 * group).astype(jnp.float32)

    live_count = intersection_list[0, 0]
    far_start = shift_tile(slice_ranges[:, 1:2], 1)[0, 0]

    def pick(slices, start, step):
        return lax.dynamic_index_in_dim(
            slices, jnp.minimum(start + step, depth - 1), 0, keepdims=False
        )

    near_start = slice_ranges[0, 0]
    right_keep = pick(right, near_start, group)
    right_send = pick(right, near_start, 1 - group)
    left_keep = pick(left, far_start, group)
    left_send = pick(left, far_start, 1 - group)
    left_got = swap_groups(left_send, members)
    far_own = shift_tile(left_keep, -1)
    right_got = swap_groups(right_send, members)
    far_other = shift_tile(left_got, -1)

    forward_np, inverse_np = row_tables(width, members)
    forward_hi, forward_lo = hi_lo(forward_np)
    table_hi = lax.dynamic_index_in_dim(forward_hi, member, 0, keepdims=False)
    table_lo = lax.dynamic_index_in_dim(forward_lo, member, 0, keepdims=False)

    def gathered(block):
        parts = [block] + [shift_members(block, members, s) for s in range(1, members)]
        if members == 2:
            first = member == 0
            ordered = [jnp.where(first, parts[0], parts[1]), jnp.where(first, parts[1], parts[0])]
            return jnp.concatenate(ordered, axis=0)
        order = (member - jnp.arange(members)) % members
        return jnp.take(jnp.stack(parts), order, axis=0).reshape(members * rows, width)

    def row_pass(block):
        pixels = gathered(block)
        spec = jnp.dot(pixels, table_hi, preferred_element_type=jnp.float32) + jnp.dot(
            pixels, table_lo, preferred_element_type=jnp.float32
        )
        return spec.reshape(2, quarter, 2 * columns)

    twist_cos, twist_sin = twist_table(height)
    forward_table = column_table(quarter, -1.0)

    def column_pass(own, other):
        even = own + other
        odd = (own - other) * sign
        er, ei = even[..., :columns], even[..., columns:]
        dr, di = odd[..., :columns], odd[..., columns:]
        parts = [
            (er[0] + er[1], ei[0] + ei[1]),
            (dr[0] + di[1], di[0] - dr[1]),
            (er[0] - er[1], ei[0] - ei[1]),
            (dr[0] - di[1], di[0] + dr[1]),
        ]
        result = []
        for r in range(4):
            turned = rotate(*parts[r], twist_cos[r], -twist_sin[r])
            spec = split(forward_table, jnp.concatenate(turned, axis=0))
            result.append((spec[:quarter], spec[quarter:]))
        return result

    near = column_pass(row_pass(right_keep), row_pass(right_got))
    far = column_pass(row_pass(far_own), row_pass(far_other))
    factor = jnp.where(group < live_count, 1.0 / live_count.astype(jnp.float32), 0.0) * (
        1.0 / math.sqrt(height * width)
    )
    k = 4 * jnp.arange(quarter, dtype=jnp.int32)[None, :] + jnp.arange(4, dtype=jnp.int32)[:, None]
    angle_k = (k * intersection_list[0, 1] % height).astype(jnp.float32) * (2.0 * math.pi / height)
    kr, ki = jnp.cos(angle_k) * factor, jnp.sin(angle_k) * factor
    l = member * columns + jnp.arange(columns, dtype=jnp.int32)
    angle_l = (l * intersection_list[0, 2] % width).astype(jnp.float32) * (2.0 * math.pi / width)
    lr, li = jnp.cos(angle_l), jnp.sin(angle_l)

    def unpack(vr, vi):
        mr, mi = mirrored(vr), mirrored(vi)
        return (
            0.5 * (vr + mr),
            0.5 * (vi - mi),
            0.5 * (vi + mi),
            0.5 * (mr - vr),
        )

    def first(spec):
        return unpack(jnp.stack([v[0][:, 0] for v in spec]), jnp.stack([v[1][:, 0] for v in spec]))

    n0r, n0i, n1r, n1i = first(near)
    f0r, f0i, f1r, f1i = first(far)
    p0r, p0i = rotate(*cross(n0r, n0i, f0r, f0i, scale), kr, ki)
    p1r, p1i = rotate(*cross(n1r, n1i, f1r, f1i, scale), kr, ki)
    nyquist = (1 - 2 * ((width // 2 * intersection_list[0, 2] % width) // (width // 2))).astype(
        jnp.float32
    )
    packed_r = p0r - p1i * nyquist
    packed_i = p0i + p1r * nyquist
    first_column = jnp.logical_and(jnp.arange(columns) == 0, member == 0)
    inverse_column = column_table(quarter, 1.0)
    ur, ui = [], []
    for r in range(4):
        pr, pi = cross(*near[r], *far[r], scale)
        pr, pi = rotate(pr, pi, kr[r][:, None], ki[r][:, None])
        pr, pi = rotate(pr, pi, lr, li)
        pr = jnp.where(first_column, packed_r[r][:, None], pr)
        pi = jnp.where(first_column, packed_i[r][:, None], pi)
        wave = split(inverse_column, jnp.concatenate([pr, pi], axis=0))
        turned = rotate(wave[:quarter], wave[quarter:], twist_cos[r], twist_sin[r])
        ur.append(turned[0])
        ui.append(turned[1])
    even = jnp.stack(
        [
            jnp.concatenate([ur[0] + ur[2], ui[0] + ui[2]], axis=-1),
            jnp.concatenate([ur[0] - ur[2], ui[0] - ui[2]], axis=-1),
        ]
    )
    odd = sign * jnp.stack(
        [
            jnp.concatenate([ur[1] + ur[3], ui[1] + ui[3]], axis=-1),
            jnp.concatenate([ui[3] - ui[1], ur[1] - ur[3]], axis=-1),
        ]
    )
    own = (even + odd).reshape(members, rows, 2 * columns)
    other = (even - odd).reshape(members, rows, 2 * columns)

    inverse_table = jnp.asarray(inverse_np.astype(np.float32))
    own_parts, other_parts = [], []
    step = rows // CHUNKS
    for c in range(CHUNKS):
        cut = slice(c * step, (c + 1) * step)
        sent = encode(other[:, cut])
        if c > 0:
            sent, got = lax.optimization_barrier((sent, got))
        got = tuple(swap_groups(v, members) for v in sent)
        total = own[:, cut] + decode(*got)
        result = None
        for s in range(members):
            target = (member + s) % members
            block = lax.dynamic_index_in_dim(total, target, 0, keepdims=False)
            if s > 0:
                block = shift_members(block, members, s)
            table = lax.dynamic_index_in_dim(
                inverse_table, (member - s) % members, 0, keepdims=False
            )
            term = jnp.dot(block, table, precision=HIGH)
            result = term if result is None else result + term
        own_parts.append(result)
        other_parts.append(decode(*[shift_tile(v, 1) for v in encode(result)]))
    return jnp.stack([jnp.concatenate(own_parts), jnp.concatenate(other_parts)])[None]


def solution(mesh):
    faces = P(("blocks", "tile"), None, "pencil", None)
    lists = P(("blocks", "tile"), None)
    return jax.shard_map(
        shards,
        mesh=mesh,
        in_specs=(faces, faces, lists, lists),
        out_specs=faces,
        check_vma=False,
    )
```

```python
import math

import jax
import jax.numpy as jnp
import ml_dtypes
import numpy as np
from jax import lax
from jax.sharding import PartitionSpec as P

REG = 0.25
CHUNKS = 2
HIGH = lax.Precision.HIGH


def shift_tile(value, steps):
    count = lax.axis_size("tile")
    return lax.ppermute(value, "tile", [(s, (s + steps) % count) for s in range(count)])


def swap_groups(value, members):
    count = 2 * members
    return lax.ppermute(value, "pencil", [(s, (s + members) % count) for s in range(count)])


def shift_members(value, members, steps):
    pairs = [
        (g * members + s, g * members + (s + steps) % members)
        for g in range(2)
        for s in range(members)
    ]
    return lax.ppermute(value, "pencil", pairs)


def hi_lo(table):
    high = table.astype(ml_dtypes.bfloat16)
    low = (table - high.astype(np.float64)).astype(ml_dtypes.bfloat16)
    return jnp.asarray(high), jnp.asarray(low)


def row_tables(width, members):
    half = width // 2
    columns = half // members
    x = np.arange(width)[:, None]
    l = np.arange(half)[None, :]
    angle = (x * l % width) * (2.0 * math.pi / width)
    cos_part, sin_part = np.cos(angle), -np.sin(angle)
    sin_part[:, 0] = 1.0 - 2.0 * (np.arange(width) % 2)
    forward = np.stack([cos_part, sin_part], axis=1)
    forward = forward.reshape(width, 2, members, columns).transpose(2, 0, 1, 3)
    forward = forward.reshape(members, width, 2 * columns)
    weight = np.where(np.arange(half) == 0, 1.0, 2.0)
    inverse = np.stack([cos_part * weight, sin_part * weight], axis=1)
    inverse = inverse.reshape(width, 2, members, columns).transpose(2, 1, 3, 0)
    inverse = inverse.reshape(members, 2 * columns, width)
    return forward, inverse


def column_table(quarter, sign):
    n = np.arange(quarter)
    angle = (n[:, None] * n[None, :] % quarter) * (2.0 * math.pi / quarter)
    c, s = np.cos(angle), sign * np.sin(angle)
    return np.block([[c, -s], [s, c]]).astype(np.float32)


def twist_table(height):
    quarter = height // 4
    angle = np.arange(4)[:, None] * np.arange(quarter)[None, :] * (2.0 * math.pi / height)
    return (
        np.cos(angle).astype(np.float32)[:, :, None],
        np.sin(angle).astype(np.float32)[:, :, None],
    )


def split(a, b):
    return jnp.dot(a, b, precision=HIGH)


def encode(value):
    tall = value.shape[-2]
    group = math.gcd(tall, 64)
    grouped = value.reshape(value.shape[:-2] + (tall // group, group, value.shape[-1]))
    peak = jnp.maximum(jnp.max(jnp.abs(grouped), axis=-2, keepdims=True), 1e-30)
    coded = jnp.round(grouped * (32767.0 / peak)).astype(jnp.int16)
    return coded.reshape(value.shape), jnp.squeeze(peak, axis=-2) * (1.0 / 32767.0)


def decode(coded, scale):
    tall = coded.shape[-2]
    count = scale.shape[-2]
    grouped = coded.reshape(coded.shape[:-2] + (count, tall // count, coded.shape[-1]))
    return (grouped.astype(jnp.float32) * scale[..., None, :]).reshape(coded.shape)


def mirrored(vec):
    turn = np.eye(vec.shape[1], dtype=np.float32)[::-1]
    flipped = jnp.dot(vec, turn, precision=lax.Precision.HIGHEST)
    rolled = jnp.dot(vec, np.roll(turn, 1, axis=1), precision=lax.Precision.HIGHEST)
    return jnp.stack([rolled[0], flipped[3], flipped[2], flipped[1]])


def cross(nr, ni, fr, fi, scale):
    pr = nr * fr + ni * fi
    pi = ni * fr - nr * fi
    weight = 1.0 / (jnp.sqrt(pr * pr + pi * pi) + scale)
    return pr * weight, pi * weight


def rotate(ar, ai, br, bi):
    return ar * br - ai * bi, ar * bi + ai * br


def shards(right_face, left_face, intersection_list, slice_ranges):
    right = right_face[0]
    left = left_face[0]
    depth, rows, width = right.shape
    count = lax.axis_size("pencil")
    members = count // 2
    height = rows * count
    quarter = height // 4
    columns = width // (2 * members)
    scale = REG * height * width
    place = lax.axis_index("pencil")
    group = place // members
    member = place % members
    sign = (1 - 2 * group).astype(jnp.float32)

    live_count = intersection_list[0, 0]
    far_start = shift_tile(slice_ranges[:, 1:2], 1)[0, 0]

    def pick(slices, start, step):
        return lax.dynamic_index_in_dim(
            slices, jnp.minimum(start + step, depth - 1), 0, keepdims=False
        )

    near_start = slice_ranges[0, 0]
    right_keep = pick(right, near_start, group)
    right_send = pick(right, near_start, 1 - group)
    left_keep = pick(left, far_start, group)
    left_send = pick(left, far_start, 1 - group)
    left_got = swap_groups(left_send, members)
    far_own = shift_tile(left_keep, -1)
    right_got = swap_groups(right_send, members)
    far_other = shift_tile(left_got, -1)

    forward_np, inverse_np = row_tables(width, members)
    forward_hi, forward_lo = hi_lo(forward_np)
    table_hi = lax.dynamic_index_in_dim(forward_hi, member, 0, keepdims=False)
    table_lo = lax.dynamic_index_in_dim(forward_lo, member, 0, keepdims=False)

    def gathered(block):
        parts = [block] + [shift_members(block, members, s) for s in range(1, members)]
        if members == 2:
            first = member == 0
            ordered = [jnp.where(first, parts[0], parts[1]), jnp.where(first, parts[1], parts[0])]
            return jnp.concatenate(ordered, axis=0)
        order = (member - jnp.arange(members)) % members
        return jnp.take(jnp.stack(parts), order, axis=0).reshape(members * rows, width)

    def row_pass(block):
        pixels = gathered(block)
        spec = jnp.dot(pixels, table_hi, preferred_element_type=jnp.float32) + jnp.dot(
            pixels, table_lo, preferred_element_type=jnp.float32
        )
        return spec

    twist_cos, twist_sin = twist_table(height)
    forward_table = column_table(quarter, -1.0)

    def column_pass(own, other):
        def cut(j, part):
            where = (slice(j * quarter, (j + 1) * quarter), slice(part * columns, (part + 1) * columns))
            a, b = own[where], other[where]
            return a + b, (a - b) * sign

        er, ei, dr, di = [None] * 2, [None] * 2, [None] * 2, [None] * 2
        for j in range(2):
            er[j], dr[j] = cut(j, 0)
            ei[j], di[j] = cut(j, 1)
        parts = [
            (er[0] + er[1], ei[0] + ei[1]),
            (dr[0] + di[1], di[0] - dr[1]),
            (er[0] - er[1], ei[0] - ei[1]),
            (dr[0] - di[1], di[0] + dr[1]),
        ]
        result = []
        for r in range(4):
            turned = rotate(*parts[r], twist_cos[r], -twist_sin[r])
            spec = split(forward_table, jnp.concatenate(turned, axis=0))
            result.append((spec[:quarter], spec[quarter:]))
        return result

    near = column_pass(row_pass(right_keep), row_pass(right_got))
    far = column_pass(row_pass(far_own), row_pass(far_other))
    factor = jnp.where(group < live_count, 1.0 / live_count.astype(jnp.float32), 0.0) * (
        1.0 / math.sqrt(height * width)
    )
    k = 4 * jnp.arange(quarter, dtype=jnp.int32)[None, :] + jnp.arange(4, dtype=jnp.int32)[:, None]
    angle_k = (k * intersection_list[0, 1] % height).astype(jnp.float32) * (2.0 * math.pi / height)
    kr, ki = jnp.cos(angle_k) * factor, jnp.sin(angle_k) * factor
    l = member * columns + jnp.arange(columns, dtype=jnp.int32)
    angle_l = (l * intersection_list[0, 2] % width).astype(jnp.float32) * (2.0 * math.pi / width)
    lr, li = jnp.cos(angle_l), jnp.sin(angle_l)

    def unpack(vr, vi):
        mr, mi = mirrored(vr), mirrored(vi)
        return (
            0.5 * (vr + mr),
            0.5 * (vi - mi),
            0.5 * (vi + mi),
            0.5 * (mr - vr),
        )

    def first(spec):
        return unpack(jnp.stack([v[0][:, 0] for v in spec]), jnp.stack([v[1][:, 0] for v in spec]))

    n0r, n0i, n1r, n1i = first(near)
    f0r, f0i, f1r, f1i = first(far)
    p0r, p0i = rotate(*cross(n0r, n0i, f0r, f0i, scale), kr, ki)
    p1r, p1i = rotate(*cross(n1r, n1i, f1r, f1i, scale), kr, ki)
    nyquist = (1 - 2 * ((width // 2 * intersection_list[0, 2] % width) // (width // 2))).astype(
        jnp.float32
    )
    packed_r = p0r - p1i * nyquist
    packed_i = p0i + p1r * nyquist
    first_column = jnp.logical_and(jnp.arange(columns) == 0, member == 0)
    inverse_column = column_table(quarter, 1.0)
    ur, ui = [], []
    for r in range(4):
        pr, pi = cross(*near[r], *far[r], scale)
        pr, pi = rotate(pr, pi, kr[r][:, None], ki[r][:, None])
        pr, pi = rotate(pr, pi, lr, li)
        pr = jnp.where(first_column, packed_r[r][:, None], pr)
        pi = jnp.where(first_column, packed_i[r][:, None], pi)
        wave = split(inverse_column, jnp.concatenate([pr, pi], axis=0))
        turned = rotate(wave[:quarter], wave[quarter:], twist_cos[r], twist_sin[r])
        ur.append(turned[0])
        ui.append(turned[1])
    even = jnp.stack(
        [
            jnp.concatenate([ur[0] + ur[2], ui[0] + ui[2]], axis=-1),
            jnp.concatenate([ur[0] - ur[2], ui[0] - ui[2]], axis=-1),
        ]
    )
    odd = sign * jnp.stack(
        [
            jnp.concatenate([ur[1] + ur[3], ui[1] + ui[3]], axis=-1),
            jnp.concatenate([ui[3] - ui[1], ur[1] - ur[3]], axis=-1),
        ]
    )
    own = (even + odd).reshape(members, rows, 2 * columns)
    other = (even - odd).reshape(members, rows, 2 * columns)

    inverse_table = jnp.asarray(inverse_np.astype(np.float32))
    own_parts, other_parts = [], []
    step = rows // CHUNKS
    for c in range(CHUNKS):
        cut = slice(c * step, (c + 1) * step)
        sent = encode(other[:, cut])
        if c > 0:
            sent, got = lax.optimization_barrier((sent, got))
        got = tuple(swap_groups(v, members) for v in sent)
        tables = inverse_table
        if c > 0:
            tables, got, result = lax.optimization_barrier((tables, got, result))
        total = own[:, cut] + decode(*got)
        result = None
        for s in range(members):
            target = (member + s) % members
            block = lax.dynamic_index_in_dim(total, target, 0, keepdims=False)
            if s > 0:
                block = shift_members(block, members, s)
            table = lax.dynamic_index_in_dim(
                tables, (member - s) % members, 0, keepdims=False
            )
            term = jnp.dot(block, table, precision=HIGH)
            result = term if result is None else result + term
        own_parts.append(result)
        other_parts.append(decode(*[shift_tile(v, 1) for v in encode(result)]))
    return jnp.stack([jnp.concatenate(own_parts), jnp.concatenate(other_parts)])[None]


def solution(mesh):
    faces = P(("blocks", "tile"), None, "pencil", None)
    lists = P(("blocks", "tile"), None)
    return jax.shard_map(
        shards,
        mesh=mesh,
        in_specs=(faces, faces, lists, lists),
        out_specs=faces,
        check_vma=False,
    )
```
